512 devices in a mesh: band: 64 (over x, y, z_lo), mem: 8 (over z_hi, core).
Axes of the slice: x: 4, y: 4, z: 16 (z_hi: 4, z_lo: 4; z = z_hi * 4 + z_lo), core: 2. Of those that a mesh axis runs over, the one named last changes fastest.
Arguments:
- perturbations: bfloat16 [80, 32, 131072], P('mem', None, 'band'), may hold values from -0.59765625 to 0.59765625
- mode_weights: bfloat16 [80, 16, 131072], P('mem', None, 'band'), may hold values from -6 to 6
- vertical_modes: bfloat16 [32, 16], replicated, may hold values from -1.5 to 1.5
- interp_weights: bfloat16 [16384, 128, 128], P(('band', 'mem')), may hold values from -1 to 2, as said below
- source_rows: int32 [16384, 128], P(('band', 'mem')), may hold values from 0 to 6143, as said below
- live_tiles: int32 [64], P('band'), may hold values from 64 to 256
- fine_cotangent: bfloat16 [32, 2097152], P(None, ('band', 'mem')), may hold values from -6 to 6
Outputs:
- fine_increment: bfloat16 [32, 2097152], P(None, ('band', 'mem'))
- mode_gradient: bfloat16 [80, 16, 131072], P('mem', None, 'band')
The draws below stay inside these ranges and needn't reach their ends.
Inputs may be any that keep to these rules, and one draw needn't show every extreme that they name: `source_rows`: the rows of one tile are distinct. `interp_weights`: each fine point's weights sum to one, and each fine point has at most 16 nonzero weights.
All inputs are finite; a program needn't handle non-finite values.
Results may differ from the reference program's by a relative error of at most 0.0049.
Values may be sent and summed in bfloat16 or wider, within the bound.
No kernel may reach another device: no remote copies, remote signals or barrier semaphores. Data moves between devices by JAX's collectives and lax.ppermute only.
A program may use at most 64 MiB of HBM per device.

```python
import jax
import jax.numpy as jnp
from jax import lax

MEMBERS = 80
LEV = 32
MODES = 16
COARSE_PER_BAND = 2048
FINE_TILE_POINTS = 128
COARSE_BLOCK = 128
LATITUDE_LENGTH = 32
TILE_BAND = 256
BANDS = 64
POINTS = 131072
TILE_SLOTS = 16384
FINE = 2097152


def column_order(key):
    key = jax.random.fold_in(key, 21)
    scores = jax.random.randint(key, (TILE_SLOTS, COARSE_BLOCK), 0, 1 << 20) * COARSE_BLOCK + jnp.arange(COARSE_BLOCK, dtype=jnp.int32)[None, :]
    return jnp.argsort(scores, axis=1).astype(jnp.int32)


def lagrange_pick(frac, row_offset):
    first = -frac * (frac - 1.0) * (frac - 2.0) / 6.0
    second = (frac + 1.0) * (frac - 1.0) * (frac - 2.0) / 2.0
    third = -(frac + 1.0) * frac * (frac - 2.0) / 2.0
    fourth = (frac + 1.0) * frac * (frac - 1.0) / 6.0
    picked = jnp.where(row_offset == 0, first, 0.0) + jnp.where(row_offset == 1, second, 0.0)
    return picked + jnp.where(row_offset == 2, third, 0.0) + jnp.where(row_offset == 3, fourth, 0.0)


def draw_interp_weights(key, part):
    order = column_order(key)
    key = jax.random.fold_in(key, 11)
    key_x, key_y = jax.random.split(key)
    frac_x = jax.random.uniform(key_x, (TILE_SLOTS, 1, FINE_TILE_POINTS), jnp.float32)
    frac_y = jax.random.uniform(key_y, (TILE_SLOTS, 1, FINE_TILE_POINTS), jnp.float32)
    grid_points = jnp.arange(FINE_TILE_POINTS, dtype=jnp.int32)
    start_index = grid_points * (LATITUDE_LENGTH - 3) // FINE_TILE_POINTS
    column_count = jnp.arange(COARSE_BLOCK, dtype=jnp.int32)
    along_column = (column_count % LATITUDE_LENGTH)[:, None] - start_index[None, :]
    across_rows = jnp.broadcast_to((column_count // LATITUDE_LENGTH)[:, None], (COARSE_BLOCK, FINE_TILE_POINTS))
    weights = lagrange_pick(frac_x, along_column[None]) * lagrange_pick(frac_y, across_rows[None])
    weights = jnp.take_along_axis(weights, order[:, :, None], axis=1)
    return weights.astype(jnp.bfloat16)


def draw_source_rows(key, part):
    order = column_order(key)
    key = jax.random.fold_in(key, 12)
    source_key, key_o = jax.random.split(key)
    step_width = jax.random.randint(source_key, (TILE_SLOTS, 1), LATITUDE_LENGTH, LATITUDE_LENGTH + COARSE_PER_BAND // 2)
    top_rows = 3 * COARSE_PER_BAND - LATITUDE_LENGTH - 3 * step_width
    row_offset = jax.random.randint(key_o, (TILE_SLOTS, 1), 0, top_rows + 1)
    row_offset = row_offset.at[0].set(0)
    row_offset = row_offset.at[TILE_SLOTS - 1].set(top_rows[TILE_SLOTS - 1])
    column_count = jnp.arange(COARSE_BLOCK, dtype=jnp.int32)[None, :]
    row_count = (row_offset + column_count % LATITUDE_LENGTH + column_count // LATITUDE_LENGTH * step_width).astype(jnp.int32)
    return jnp.take_along_axis(row_count, order, axis=1).astype(jnp.int32)


def draw_live_tiles(key, part):
    key = jax.random.fold_in(key, 13)
    key_c, key_a, key_b = jax.random.split(key, 3)
    counts = jax.random.randint(key_c, (BANDS,), TILE_BAND // 4, TILE_BAND + 1)
    fullest = jax.random.randint(key_a, (), 0, BANDS)
    emptiest = (fullest + jax.random.randint(key_b, (), 1, BANDS)) % BANDS
    counts = counts.at[fullest].set(TILE_BAND).at[emptiest].set(TILE_BAND // 4)
    return counts.astype(jnp.int32)


def block_levels(rng, shape, shards, least, high):
    level = 1.0
    for axis_at, blocks in shards:
        steps = jax.random.uniform(jax.random.fold_in(jax.random.fold_in(rng, 6), axis_at), (blocks,), jnp.float32, least / len(shards), high / len(shards))
        level = level * jnp.repeat(jnp.exp(steps), shape[axis_at] // blocks).reshape((-1,) + (1,) * (len(shape) - 1 - axis_at))
    return level


def centred(rng, extent, deviation, limit, cuts=(), kind=jnp.bfloat16):
    factor_of = block_levels(rng, extent, cuts, -0.22, 0.18) if cuts else 1.0
    result = jax.random.normal(rng, extent, jnp.float32) * deviation * factor_of
    return jnp.minimum(jnp.maximum(result, -limit), limit).astype(kind)


def setup_inputs(seed: int = 0) -> dict:
    keys = jax.random.split(jax.random.key(seed), 8)
    perturbations = centred(keys[0], (MEMBERS, LEV, POINTS), 0.1, 0.59765625, ((0, 8), (2, 64)))
    mode_weights = centred(keys[1], (MEMBERS, MODES, POINTS), 1.0, 6.0, ((0, 8), (2, 64)))
    vertical_modes = centred(keys[2], (LEV, MODES), MODES ** -0.5, 1.5)
    interp_weights = draw_interp_weights(jax.random.fold_in(keys[7], 71), 0)
    source_rows = draw_source_rows(jax.random.fold_in(keys[7], 71), 0)
    live_tiles = draw_live_tiles(jax.random.fold_in(keys[7], 71), 0)
    fine_cotangent = centred(keys[6], (LEV, FINE), 1.0, 6.0, ((1, 512),))
    return {"perturbations": perturbations, "mode_weights": mode_weights, "vertical_modes": vertical_modes, "interp_weights": interp_weights, "source_rows": source_rows, "live_tiles": live_tiles, "fine_cotangent": fine_cotangent}


def reference(perturbations, mode_weights, vertical_modes, interp_weights, source_rows, live_tiles, fine_cotangent):

    def member_term(total, pair):
        member_x, member_a = pair
        alpha = jnp.dot(vertical_modes, member_a, preferred_element_type=jnp.float32)
        return (total + member_x.astype(jnp.float32) * alpha, None)
    coarse, _ = lax.scan(member_term, jnp.zeros((LEV, POINTS), jnp.float32), (perturbations, mode_weights))
    padded = jnp.pad(coarse, ((0, 0), (COARSE_PER_BAND, COARSE_PER_BAND))).astype(jnp.bfloat16)
    weights_b = interp_weights.reshape(BANDS, TILE_BAND, COARSE_BLOCK, FINE_TILE_POINTS)
    rows_b = source_rows.reshape(BANDS, TILE_BAND, COARSE_BLOCK)
    cot_b = fine_cotangent.reshape(LEV, BANDS, TILE_BAND, FINE_TILE_POINTS).transpose(1, 0, 2, 3)

    def band_work(args):
        band, weights, row_count, cot, live = args
        extended = lax.dynamic_slice_in_dim(padded, (band * COARSE_PER_BAND).astype(jnp.int32), 3 * COARSE_PER_BAND, 1)
        block = extended[:, row_count].astype(jnp.float32)
        keep = (jnp.arange(TILE_BAND, dtype=jnp.int32) < live).astype(jnp.float32)
        wide_w = weights.astype(jnp.float32)
        fine = jnp.einsum('ltc,tcf->ltf', block, wide_w) * keep[None, :, None]
        masked = cot.astype(jnp.float32) * keep[None, :, None]
        back = jnp.einsum('ltf,tcf->ltc', masked, wide_w)
        ext_adj = jnp.zeros((LEV, 3 * COARSE_PER_BAND), jnp.float32).at[:, row_count.reshape(-1)].add(back.reshape(LEV, -1))
        return (fine.astype(jnp.bfloat16), ext_adj)
    bands = jnp.arange(BANDS, dtype=jnp.int32)
    fine_b, ext_b = lax.map(band_work, (bands, weights_b, rows_b, cot_b, live_tiles))
    fine_increment = fine_b.transpose(1, 0, 2, 3).reshape(LEV, FINE)
    pieces = ext_b.reshape(BANDS, LEV, 3, COARSE_PER_BAND)
    gathered = jnp.zeros((LEV, BANDS + 2, COARSE_PER_BAND), jnp.float32)
    for row_offset in range(3):
        gathered = gathered.at[:, row_offset:row_offset + BANDS].add(pieces[:, :, row_offset].transpose(1, 0, 2))
    adjoint = gathered[:, 1:BANDS + 1].reshape(LEV, POINTS)
    modes_wide = vertical_modes.astype(jnp.float32)

    def member_grad(member_x):
        product = member_x.astype(jnp.float32) * adjoint
        return jnp.dot(modes_wide.T, product, precision=lax.Precision.HIGHEST).astype(jnp.bfloat16)
    mode_gradient = lax.map(member_grad, perturbations)
    return (fine_increment, mode_gradient)
```

```python
import functools

import jax
import jax.numpy as jnp
from jax import lax
from jax.experimental import pallas as pl
from jax.experimental.pallas import tpu as pltpu
from jax.sharding import PartitionSpec as P

F32 = jnp.float32
BF16 = jnp.bfloat16
LANES = 256
BAND = 2048
CHUNKS = BAND // LANES
GROUP = 8


def scatter_kernel(live_ref, rows_ref, weights_ref, cot_ref, out_ref):
    tiles, width, _ = weights_ref.shape
    levels = cot_ref.shape[0]
    chunks = out_ref.shape[0] // levels
    first = lax.axis_index("mem") * tiles
    live = live_ref[0]
    lane = lax.broadcasted_iota(jnp.int32, (width, LANES), 1)
    turned = rows_ref[...].T
    for start in range(0, tiles, GROUP):
        spread, hot = [], []
        for tile in range(start, start + GROUP):
            cot = cot_ref[:, tile * width : (tile + 1) * width]
            back = lax.dot_general(
                cot, weights_ref[tile], (((1,), (1,)), ((), ())), preferred_element_type=F32
            )
            back = jnp.where(first + tile < live, back, 0.0)
            chunk = rows_ref[tile : tile + 1, :] // LANES
            spread.append(
                jnp.concatenate(
                    [jnp.where(chunk == k, back, 0.0).astype(BF16) for k in range(chunks)], axis=0
                )
            )
            column = turned[:, tile : tile + 1] % LANES
            hot.append(jnp.where(column == lane, 1.0, 0.0).astype(BF16))
        part = jnp.dot(
            jnp.concatenate(spread, axis=1),
            jnp.concatenate(hot, axis=0),
            preferred_element_type=F32,
        )
        if start == 0:
            total = part
        else:
            total = total + part
    out_ref[...] = total.astype(BF16)


def scatter(live_tiles, source_rows, interp_weights, fine_cotangent):
    levels = fine_cotangent.shape[0]
    vmem = pl.BlockSpec(memory_space=pltpu.VMEM)
    return pl.pallas_call(
        scatter_kernel,
        out_shape=jax.ShapeDtypeStruct((3 * CHUNKS * levels, LANES), BF16),
        in_specs=[pl.BlockSpec(memory_space=pltpu.SMEM), vmem, vmem, vmem],
        out_specs=vmem,
        compiler_params=pltpu.CompilerParams(vmem_limit_bytes=40 * 2**20),
        cost_estimate=pl.CostEstimate(flops=2 * 10**9, bytes_accessed=2 * 10**6, transcendentals=0),
        name="scatter",
    )(live_tiles, source_rows, interp_weights, fine_cotangent)


def partial_kernel(pert_ref, weights_ref, modes_ref, out_ref):
    members, levels, points = pert_ref.shape
    for chunk in range(points // LANES):
        at = slice(chunk * LANES, (chunk + 1) * LANES)
        total = jnp.zeros((levels, LANES), F32)
        for k in range(members):
            alpha = jnp.dot(modes_ref[...], weights_ref[k, :, at], preferred_element_type=F32)
            total = total + pert_ref[k, :, at].astype(F32) * alpha
        out_ref[chunk * levels : (chunk + 1) * levels, :] = total.astype(BF16)


def partial_sum(perturbations, mode_weights, vertical_modes):
    members, levels, points = perturbations.shape
    vmem = pl.BlockSpec(memory_space=pltpu.VMEM)
    return pl.pallas_call(
        partial_kernel,
        out_shape=jax.ShapeDtypeStruct((points // LANES * levels, LANES), BF16),
        in_specs=[vmem, vmem, vmem],
        out_specs=vmem,
        compiler_params=pltpu.CompilerParams(vmem_limit_bytes=40 * 2**20),
        cost_estimate=pl.CostEstimate(flops=2 * 10**9, bytes_accessed=3 * 10**6, transcendentals=0),
        name="partial_sum",
    )(perturbations, mode_weights, vertical_modes)


def fine_kernel(live_ref, rows_ref, weights_ref, middle_ref, sides_ref, out_ref):
    tiles, width, _ = weights_ref.shape
    levels = out_ref.shape[0]
    first = lax.axis_index("mem") * tiles
    live = live_ref[0]
    line = lax.broadcasted_iota(jnp.int32, (LANES, 2 * width), 0)
    extended = jnp.concatenate([sides_ref[0], middle_ref[...], sides_ref[1]], axis=0)
    for tile in range(0, tiles, 2):
        rows = jnp.concatenate([rows_ref[tile : tile + 1, :], rows_ref[tile + 1 : tile + 2, :]], axis=1)
        chunk, column = rows // LANES, rows % LANES
        hot = jnp.where(column == line, 1.0, 0.0).astype(BF16)
        picked = jnp.dot(extended, hot, preferred_element_type=F32)
        block = jnp.zeros((levels, 2 * width), F32)
        for k in range(extended.shape[0] // levels):
            block = jnp.where(chunk == k, picked[k * levels : (k + 1) * levels], block)
        block = block.astype(BF16)
        for i in range(2):
            fine = jnp.dot(
                block[:, i * width : (i + 1) * width], weights_ref[tile + i], preferred_element_type=F32
            )
            fine = jnp.where(first + tile + i < live, fine, 0.0)
            out_ref[:, (tile + i) * width : (tile + i + 1) * width] = fine.astype(BF16)


def fine_sum(live_tiles, source_rows, interp_weights, middle, sides):
    tiles, width, _ = interp_weights.shape
    levels = middle.shape[0] // CHUNKS
    vmem = pl.BlockSpec(memory_space=pltpu.VMEM)
    return pl.pallas_call(
        fine_kernel,
        out_shape=jax.ShapeDtypeStruct((levels, tiles * width), BF16),
        in_specs=[pl.BlockSpec(memory_space=pltpu.SMEM), vmem, vmem, vmem, vmem],
        out_specs=vmem,
        compiler_params=pltpu.CompilerParams(vmem_limit_bytes=40 * 2**20),
        cost_estimate=pl.CostEstimate(flops=2 * 10**9, bytes_accessed=2 * 10**6, transcendentals=0),
        name="fine_sum",
    )(live_tiles, source_rows, interp_weights, middle, sides)


def gradient_kernel(pert_ref, modes_ref, adjoint_ref, out_ref):
    members, levels, points = pert_ref.shape
    modes = jnp.concatenate([modes_ref[...], modes_ref[...]], axis=0)
    for chunk in range(points // LANES):
        at = slice(chunk * LANES, (chunk + 1) * LANES)
        adjoint = adjoint_ref[chunk * levels : (chunk + 1) * levels, :].astype(F32)
        for k in range(members):
            product = pert_ref[k, :, at].astype(F32) * adjoint
            high = product.astype(BF16)
            low = (product - high.astype(F32)).astype(BF16)
            both = jnp.concatenate([high, low], axis=0)
            out_ref[k, :, at] = lax.dot_general(
                modes, both, (((0,), (0,)), ((), ())), preferred_element_type=F32
            ).astype(BF16)


def gradient(perturbations, vertical_modes, adjoint):
    members, levels, points = perturbations.shape
    vmem = pl.BlockSpec(memory_space=pltpu.VMEM)
    return pl.pallas_call(
        gradient_kernel,
        out_shape=jax.ShapeDtypeStruct((members, vertical_modes.shape[1], points), BF16),
        in_specs=[vmem, vmem, vmem],
        out_specs=vmem,
        compiler_params=pltpu.CompilerParams(vmem_limit_bytes=40 * 2**20),
        cost_estimate=pl.CostEstimate(flops=2 * 10**9, bytes_accessed=3 * 10**6, transcendentals=0),
        name="gradient",
    )(perturbations, vertical_modes, adjoint)


def shards(
    perturbations,
    mode_weights,
    vertical_modes,
    interp_weights,
    source_rows,
    live_tiles,
    fine_cotangent,
):
    bands, mems = lax.axis_size("band"), lax.axis_size("mem")
    core = lax.axis_index("mem") % 2
    pairs = [[m, m + 1] for m in range(0, mems, 2)]
    chips = [list(range(c, mems, 2)) for c in range(2)]
    route = [
        (b * mems + m, (b + 1 - 2 * (m % 2)) * mems + m)
        for b in range(bands)
        for m in range(mems)
        if 0 <= b + 1 - 2 * (m % 2) < bands
    ]
    to_pair = functools.partial(lax.all_gather, axis_name="mem", axis_index_groups=pairs)
    to_chips = functools.partial(lax.all_gather, axis_name="mem", axis_index_groups=chips)
    to_bands = functools.partial(lax.ppermute, axis_name=("band", "mem"), perm=route)

    local = scatter(live_tiles, source_rows, interp_weights, fine_cotangent)
    both = to_pair(local)
    rows = local.shape[0] // 3
    here = both[0].astype(F32) + both[1].astype(F32)
    send = lax.dynamic_slice_in_dim(here, (1 - core) * 2 * rows, rows, 0).astype(BF16)
    centre = here[rows : 2 * rows]
    came = to_bands(send)
    part = partial_sum(perturbations, mode_weights, vertical_modes)
    both = to_pair(jnp.stack([part, came])).astype(F32)
    half = rows // 2
    both = lax.dynamic_slice_in_dim(both, core * half, half, 2)
    centre = lax.dynamic_slice_in_dim(centre, core * half, half, 0)
    sums = jnp.stack([both[0, 0] + both[1, 0], both[0, 1] + both[1, 1] + centre]).astype(BF16)
    sums = jnp.sum(to_chips(sums).astype(F32), axis=0).astype(BF16)
    both = to_pair(sums)
    middle = both[:, 0].reshape(rows, LANES)
    adjoint = both[:, 1].reshape(rows, LANES)
    came = to_bands(middle)
    mode_gradient = gradient(perturbations, vertical_modes, adjoint)
    sides = to_pair(came)
    fine_increment = fine_sum(live_tiles, source_rows, interp_weights, middle, sides)
    return (fine_increment, mode_gradient)


def solution(mesh):
    placed = (
        P("mem", None, "band"),
        P("mem", None, "band"),
        P(),
        P(("band", "mem"), None, None),
        P(("band", "mem"), None),
        P("band"),
        P(None, ("band", "mem")),
    )
    return jax.shard_map(
        shards,
        mesh=mesh,
        in_specs=placed,
        out_specs=(P(None, ("band", "mem")), P("mem", None, "band")),
        check_vma=False,
    )
```

```python
import functools

import jax
import jax.numpy as jnp
from jax import lax
from jax.experimental import pallas as pl
from jax.experimental.pallas import tpu as pltpu
from jax.sharding import PartitionSpec as P

F32 = jnp.float32
BF16 = jnp.bfloat16
LANES = 256
BAND = 2048
CHUNKS = BAND // LANES
GROUP = 8
STEP = 4
NEAR = 4

CENTRE = range(CHUNKS, 2 * CHUNKS)
SIDES = [*range(CHUNKS), *range(2 * CHUNKS, 3 * CHUNKS)]


def compiled(kernel, out, in_specs, name, scratch=(), flops=2 * 10**9, mib=32):
    vmem = pl.BlockSpec(memory_space=pltpu.VMEM)
    return pl.pallas_call(
        kernel,
        out_shape=out,
        in_specs=in_specs,
        out_specs=jax.tree.map(lambda _: vmem, out),
        scratch_shapes=list(scratch),
        compiler_params=pltpu.CompilerParams(vmem_limit_bytes=int(mib * 2**20)),
        cost_estimate=pl.CostEstimate(flops=flops, bytes_accessed=2 * 10**6, transcendentals=0),
        name=name,
    )


def some_rows(rows_ref, tile, count):
    return jnp.concatenate([rows_ref[t : t + 1, :] for t in range(tile, tile + count)], axis=1)


def one_hot(rows):
    line = lax.broadcasted_iota(jnp.int32, (LANES, rows.shape[1]), 0).astype(F32).astype(BF16)
    column = (rows % LANES).astype(F32).astype(BF16)
    return jnp.where(column == line, jnp.ones((), BF16), jnp.zeros((), BF16))


def scattered(rows_ref, back_ref, chunks):
    tiles, width = rows_ref.shape
    zero = jnp.zeros((), BF16)
    total = None
    for start in range(0, tiles, GROUP):
        rows = some_rows(rows_ref, start, GROUP)
        chunk = (rows // LANES).astype(F32).astype(BF16)
        back = back_ref[:, start * width : (start + GROUP) * width]
        spread = jnp.concatenate([jnp.where(chunk == k, back, zero) for k in chunks], axis=0)
        part = lax.dot_general(
            spread, one_hot(rows), (((1,), (1,)), ((), ())), preferred_element_type=F32
        )
        total = part if total is None else total + part
    return total.astype(BF16)


def back_kernel(
    live_hbm, cot_hbm, weights_hbm, back_ref, kept_ref, live_ref, cot_ref, weights_ref, sems
):
    tiles, width, _ = weights_ref.shape
    copies = [
        pltpu.make_async_copy(live_hbm, live_ref, sems.at[0]),
        pltpu.make_async_copy(cot_hbm, cot_ref, sems.at[1]),
    ]
    starts = range(0, tiles, GROUP)
    for i, start in enumerate(starts):
        at = pl.ds(start, GROUP)
        copies.append(pltpu.make_async_copy(weights_hbm.at[at], weights_ref.at[at], sems.at[2 + i]))
    for copy in copies:
        copy.start()
    copies[0].wait()
    first = lax.axis_index("mem") * tiles
    live = live_ref[0, 0]
    kept_ref[...] = jnp.full(kept_ref.shape, live - first, jnp.int32)
    copies[1].wait()
    for i, start in enumerate(starts):
        copies[2 + i].wait()
        for tile in range(start, start + GROUP):
            at = slice(tile * width, (tile + 1) * width)
            back = lax.dot_general(
                weights_ref[tile], cot_ref[:, at], (((1,), (1,)), ((), ())), preferred_element_type=F32
            ).T
            back_ref[:, at] = jnp.where(first + tile < live, back, 0.0).astype(BF16)


def back_blocks(live, cot, weights):
    hbm = pl.BlockSpec(memory_space=pltpu.HBM)
    out = (
        jax.ShapeDtypeStruct(cot.shape, BF16),
        jax.ShapeDtypeStruct((8, weights.shape[2]), jnp.int32),
    )
    live = live.reshape(1, 1)
    scratch = [
        pltpu.SMEM(live.shape, live.dtype),
        pltpu.VMEM(cot.shape, cot.dtype),
        pltpu.VMEM(weights.shape, weights.dtype),
        pltpu.SemaphoreType.DMA((2 + weights.shape[0] // GROUP,)),
    ]
    return compiled(back_kernel, out, [hbm] * 3, "back_blocks", scratch, mib=53.55)(live, cot, weights)


def sides_kernel(rows_ref, back_ref, out_ref):
    out_ref[...] = scattered(rows_ref, back_ref, SIDES)


def sides_sums(rows, back):
    vmem = pl.BlockSpec(memory_space=pltpu.VMEM)
    out = jax.ShapeDtypeStruct((len(SIDES) * back.shape[0], LANES), BF16)
    return compiled(sides_kernel, out, [vmem, vmem], "sides_sums")(rows, back)


def inner_kernel(pert_ref, weights_ref, modes_ref, rows_ref, back_ref, out_ref):
    members, levels, points = pert_ref.shape
    for chunk in range(CHUNKS):
        at = slice(chunk * LANES, (chunk + 1) * LANES)
        total = jnp.zeros((levels, LANES), F32)
        for k in range(members):
            alpha = lax.dot_general(
                modes_ref[...],
                weights_ref[k, :, at],
                (((0,), (0,)), ((), ())),
                preferred_element_type=F32,
            )
            total = total + pert_ref[k, :, at].astype(F32) * alpha
        out_ref[chunk * levels : (chunk + 1) * levels, :] = total.astype(BF16)
    out_ref[CHUNKS * levels :, :] = scattered(rows_ref, back_ref, CENTRE)


def inner_sums(pert, mode_weights, modes, rows, back):
    vmem = pl.BlockSpec(memory_space=pltpu.VMEM)
    out = jax.ShapeDtypeStruct((2 * CHUNKS * pert.shape[1], LANES), BF16)
    return compiled(inner_kernel, out, [vmem] * 5, "inner_sums")(pert, mode_weights, modes, rows, back)


def add(*refs):
    return functools.reduce(jnp.add, [ref.astype(F32) for ref in refs])


def outward_kernel(both_ref, out_ref):
    size = out_ref.shape[0]
    core = lax.axis_index("mem") % 2
    at = pl.ds(pl.multiple_of((1 - core) * size, size), size)
    out_ref[...] = add(both_ref[0, at, :], both_ref[1, at, :]).astype(BF16)


def outward(both):
    vmem = pl.BlockSpec(memory_space=pltpu.VMEM)
    out = jax.ShapeDtypeStruct((both.shape[1] // 2, LANES), BF16)
    return compiled(outward_kernel, out, [vmem], "outward", flops=10**6)(both)


def chip_kernel(inner_ref, came_ref, out_ref):
    size = came_ref.shape[1]
    half = size // 2
    core = lax.axis_index("mem") % 2
    here = pl.ds(pl.multiple_of(core * half, half), half)
    centre = pl.ds(pl.multiple_of(size + core * half, half), half)
    out_ref[:half, :] = add(inner_ref[0, here, :], inner_ref[1, here, :]).astype(BF16)
    out_ref[half:, :] = add(
        inner_ref[0, centre, :], inner_ref[1, centre, :], came_ref[0, here, :], came_ref[1, here, :]
    ).astype(BF16)


def chip_sums(inner, came):
    vmem = pl.BlockSpec(memory_space=pltpu.VMEM)
    out = jax.ShapeDtypeStruct(came.shape[1:], BF16)
    return compiled(chip_kernel, out, [vmem, vmem], "chip_sums", flops=10**6)(inner, came)


def total_kernel(parts_ref, out_ref):
    out_ref[...] = add(*[parts_ref[i] for i in range(parts_ref.shape[0])]).astype(BF16)


def totals(parts):
    vmem = pl.BlockSpec(memory_space=pltpu.VMEM)
    out = jax.ShapeDtypeStruct(parts.shape[1:], BF16)
    return compiled(total_kernel, out, [vmem], "totals", flops=10**6)(parts)


def middle_kernel(both_ref, out_ref):
    half = both_ref.shape[1] // 2
    out_ref[:half, :] = both_ref[0, :half, :]
    out_ref[half:, :] = both_ref[1, :half, :]


def middle_of(both):
    vmem = pl.BlockSpec(memory_space=pltpu.VMEM)
    out = jax.ShapeDtypeStruct(both.shape[1:], BF16)
    return compiled(middle_kernel, out, [vmem], "middle", flops=10**6)(both)


def pick(table, rows, block, chunks):
    levels = block.shape[0]
    picked = jnp.dot(table, one_hot(rows), preferred_element_type=F32)
    chunk = rows // LANES
    for i, k in enumerate(chunks):
        block = jnp.where(chunk == k, picked[i * levels : (i + 1) * levels], block)
    return block.astype(BF16)


def centre_kernel(rows_ref, middle_ref, out_ref):
    tiles, width = rows_ref.shape
    for tile in range(0, tiles, STEP):
        at = slice(tile * width, (tile + STEP) * width)
        none = jnp.zeros((out_ref.shape[0], STEP * width), F32)
        rows = some_rows(rows_ref, tile, STEP)
        out_ref[:, at] = pick(middle_ref[...], rows, none, CENTRE)


def centre_blocks(rows, middle):
    vmem = pl.BlockSpec(memory_space=pltpu.VMEM)
    out = jax.ShapeDtypeStruct((middle.shape[0] // CHUNKS, rows.size), BF16)
    return compiled(centre_kernel, out, [vmem, vmem], "centre_blocks")(rows, middle)


def fine_kernel(kept_ref, rows_ref, weights_ref, centre_ref, sides_ref, out_ref, block_ref):
    tiles, width, _ = weights_ref.shape
    kept = kept_ref[:1, :]
    sides = jnp.concatenate([sides_ref[0], sides_ref[1]], axis=0)
    for tile in range(0, tiles, STEP):
        at = slice(tile * width, (tile + STEP) * width)
        rows = some_rows(rows_ref, tile, STEP)
        block_ref[:, at] = pick(sides, rows, centre_ref[:, at].astype(F32), SIDES)
    for tile in range(tiles):
        at = slice(tile * width, (tile + 1) * width)
        fine = jnp.dot(block_ref[:, at], weights_ref[tile], preferred_element_type=F32)
        out_ref[:, at] = jnp.where(tile < kept, fine, 0.0).astype(BF16)


def fine_sum(kept, rows, weights, blocks, sides):
    vmem = pl.BlockSpec(memory_space=pltpu.VMEM)
    out = jax.ShapeDtypeStruct(blocks.shape, BF16)
    scratch = [pltpu.VMEM(blocks.shape, BF16)]
    return compiled(fine_kernel, out, [vmem] * 5, "fine_sum", scratch)(kept, rows, weights, blocks, sides)


def gradient_kernel(pert_ref, modes_ref, both_ref, out_ref):
    members, levels, points = pert_ref.shape
    half = both_ref.shape[1] // 2
    modes = jnp.concatenate([modes_ref[...], modes_ref[...]], axis=1)
    chunks = points // LANES
    for chunk in range(chunks):
        at = slice(chunk * LANES, (chunk + 1) * LANES)
        side, row = divmod(chunk * levels, half)
        adjoint = both_ref[side, half + row : half + row + levels, :].astype(F32)
        for k in range(members):
            product = pert_ref[k, :, at].astype(F32) * adjoint
            high = product.astype(BF16)
            low = (product - high.astype(F32)).astype(BF16)
            both = jnp.concatenate([high, low], axis=0)
            out_ref[k, :, at] = jnp.dot(modes, both, preferred_element_type=F32).astype(BF16)


def gradient(pert, modes, both):
    members, levels, points = pert.shape
    vmem = pl.BlockSpec(memory_space=pltpu.VMEM)
    out = jax.ShapeDtypeStruct((members, modes.shape[0], points), BF16)
    return compiled(gradient_kernel, out, [vmem, vmem, vmem], "gradient")(pert, modes, both)


def halo_route(bands, mems, near):
    route = []
    for b in range(bands):
        for m in range(mems):
            step = 1 - 2 * (m % 2)
            to = b + step
            if 0 <= to < bands:
                turn = 2 * step if to // near != b // near else 0
                route.append((b * mems + m, to * mems + (m + turn) % mems))
    return route


def shards(
    perturbations,
    mode_weights,
    vertical_modes,
    interp_weights,
    source_rows,
    live_tiles,
    fine_cotangent,
):
    bands, mems = lax.axis_size("band"), lax.axis_size("mem")
    pairs = [[m, m + 1] for m in range(0, mems, 2)]
    chips = [list(range(c, mems, 2)) for c in range(2)]
    to_pair = functools.partial(lax.all_gather, axis_name="mem", axis_index_groups=pairs)
    to_chips = functools.partial(lax.all_gather, axis_name="mem", axis_index_groups=chips)
    to_bands = functools.partial(
        lax.ppermute, axis_name=("band", "mem"), perm=halo_route(bands, mems, NEAR)
    )

    modes = vertical_modes.T
    back, kept = back_blocks(live_tiles, fine_cotangent, interp_weights)
    came = to_bands(outward(to_pair(sides_sums(source_rows, back))))
    inner = to_pair(inner_sums(perturbations, mode_weights, modes, source_rows, back))
    sums = totals(to_chips(chip_sums(inner, to_pair(came))))
    both = to_pair(sums)
    middle = middle_of(both)
    came = to_bands(middle)
    mode_gradient = gradient(perturbations, modes, both)
    blocks = centre_blocks(source_rows, middle)
    fine_increment = fine_sum(kept, source_rows, interp_weights, blocks, to_pair(came))
    return (fine_increment, mode_gradient)


def solution(mesh):
    placed = (
        P("mem", None, "band"),
        P("mem", None, "band"),
        P(),
        P(("band", "mem"), None, None),
        P(("band", "mem"), None),
        P("band"),
        P(None, ("band", "mem")),
    )
    return jax.shard_map(
        shards,
        mesh=mesh,
        in_specs=placed,
        out_specs=(P(None, ("band", "mem")), P("mem", None, "band")),
        check_vma=False,
    )
```

```python
import functools

import jax
import jax.numpy as jnp
from jax import lax
from jax.experimental import pallas as pl
from jax.experimental.pallas import tpu as pltpu
from jax.sharding import PartitionSpec as P

F32 = jnp.float32
BF16 = jnp.bfloat16
LANES = 256
BAND = 2048
CHUNKS = BAND // LANES
GROUP = 8
STEP = 4
NEAR = 4

CENTRE = range(CHUNKS, 2 * CHUNKS)
SIDES = [*range(CHUNKS), *range(2 * CHUNKS, 3 * CHUNKS)]


def compiled(kernel, out, in_specs, name, scratch=(), flops=2 * 10**9, mib=32):
    vmem = pl.BlockSpec(memory_space=pltpu.VMEM)
    return pl.pallas_call(
        kernel,
        out_shape=out,
        in_specs=in_specs,
        out_specs=jax.tree.map(lambda _: vmem, out),
        scratch_shapes=list(scratch),
        compiler_params=pltpu.CompilerParams(vmem_limit_bytes=int(mib * 2**20)),
        cost_estimate=pl.CostEstimate(flops=flops, bytes_accessed=2 * 10**6, transcendentals=0),
        name=name,
    )


def some_rows(rows_ref, tile, count):
    return jnp.concatenate([rows_ref[t : t + 1, :] for t in range(tile, tile + count)], axis=1)


def one_hot(rows):
    line = lax.broadcasted_iota(jnp.int32, (LANES, rows.shape[1]), 0).astype(F32).astype(BF16)
    column = (rows % LANES).astype(F32).astype(BF16)
    return jnp.where(column == line, jnp.ones((), BF16), jnp.zeros((), BF16))


def scattered(rows_ref, back_ref, chunks):
    tiles, width = rows_ref.shape
    zero = jnp.zeros((), BF16)
    total = None
    for start in range(0, tiles, GROUP):
        rows = some_rows(rows_ref, start, GROUP)
        chunk = (rows // LANES).astype(F32).astype(BF16)
        back = back_ref[:, start * width : (start + GROUP) * width]
        spread = jnp.concatenate([jnp.where(chunk == k, back, zero) for k in chunks], axis=0)
        part = lax.dot_general(
            spread, one_hot(rows), (((1,), (1,)), ((), ())), preferred_element_type=F32
        )
        total = part if total is None else total + part
    return total


def back_kernel(
    live_hbm, cot_hbm, weights_hbm, back_ref, kept_ref, live_ref, cot_ref, weights_ref, sems
):
    tiles, width, _ = weights_ref.shape
    copies = [
        pltpu.make_async_copy(live_hbm, live_ref, sems.at[0]),
        pltpu.make_async_copy(cot_hbm, cot_ref, sems.at[1]),
    ]
    starts = range(0, tiles, GROUP)
    for i, start in enumerate(starts):
        at = pl.ds(start, GROUP)
        copies.append(pltpu.make_async_copy(weights_hbm.at[at], weights_ref.at[at], sems.at[2 + i]))
    for copy in copies:
        copy.start()
    copies[0].wait()
    first = lax.axis_index("mem") * tiles
    live = live_ref[0, 0]
    kept_ref[...] = jnp.full(kept_ref.shape, live - first, jnp.int32)
    copies[1].wait()
    for i, start in enumerate(starts):
        copies[2 + i].wait()
        for tile in range(start, start + GROUP):
            at = slice(tile * width, (tile + 1) * width)
            back = lax.dot_general(
                weights_ref[tile], cot_ref[:, at], (((1,), (1,)), ((), ())), preferred_element_type=F32
            ).T
            back_ref[:, at] = jnp.where(first + tile < live, back, 0.0).astype(BF16)


def back_blocks(live, cot, weights):
    hbm = pl.BlockSpec(memory_space=pltpu.HBM)
    out = (
        jax.ShapeDtypeStruct(cot.shape, BF16),
        jax.ShapeDtypeStruct((8, weights.shape[2]), jnp.int32),
    )
    live = live.reshape(1, 1)
    scratch = [
        pltpu.SMEM(live.shape, live.dtype),
        pltpu.VMEM(cot.shape, cot.dtype),
        pltpu.VMEM(weights.shape, weights.dtype),
        pltpu.SemaphoreType.DMA((2 + weights.shape[0] // GROUP,)),
    ]
    return compiled(back_kernel, out, [hbm] * 3, "back_blocks", scratch, mib=53.55)(live, cot, weights)


def sides_kernel(rows_ref, back_ref, out_ref):
    out_ref[...] = scattered(rows_ref, back_ref, SIDES).astype(BF16)


def sides_sums(rows, back):
    vmem = pl.BlockSpec(memory_space=pltpu.VMEM)
    out = jax.ShapeDtypeStruct((len(SIDES) * back.shape[0], LANES), BF16)
    return compiled(sides_kernel, out, [vmem, vmem], "sides_sums")(rows, back)


def inner_kernel(pert_ref, weights_ref, modes_ref, rows_ref, back_ref, out_ref, own_ref):
    members, levels, points = pert_ref.shape
    for chunk in range(CHUNKS):
        at = slice(chunk * LANES, (chunk + 1) * LANES)
        total = jnp.zeros((levels, LANES), F32)
        for k in range(members):
            alpha = lax.dot_general(
                modes_ref[...],
                weights_ref[k, :, at],
                (((0,), (0,)), ((), ())),
                preferred_element_type=F32,
            )
            total = total + pert_ref[k, :, at].astype(F32) * alpha
        own_ref[chunk * levels : (chunk + 1) * levels, :] = total
    own_ref[CHUNKS * levels :, :] = scattered(rows_ref, back_ref, CENTRE)
    out_ref[...] = own_ref[...].astype(BF16)


def inner_sums(pert, mode_weights, modes, rows, back):
    vmem = pl.BlockSpec(memory_space=pltpu.VMEM)
    shape = (2 * CHUNKS * pert.shape[1], LANES)
    out = (jax.ShapeDtypeStruct(shape, BF16), jax.ShapeDtypeStruct(shape, F32))
    return compiled(inner_kernel, out, [vmem] * 5, "inner_sums")(pert, mode_weights, modes, rows, back)


def add(*refs):
    return functools.reduce(jnp.add, [ref.astype(F32) for ref in refs])


def outward_kernel(both_ref, out_ref):
    size = out_ref.shape[0]
    core = lax.axis_index("mem") % 2
    at = pl.ds(pl.multiple_of((1 - core) * size, size), size)
    out_ref[...] = add(both_ref[0, at, :], both_ref[1, at, :]).astype(BF16)


def outward(both):
    vmem = pl.BlockSpec(memory_space=pltpu.VMEM)
    out = jax.ShapeDtypeStruct((both.shape[1] // 2, LANES), BF16)
    return compiled(outward_kernel, out, [vmem], "outward", flops=10**6)(both)


def chip_kernel(inner_ref, own_ref, came_ref, out_ref, exact_ref):
    size = came_ref.shape[1]
    half = size // 2
    core = lax.axis_index("mem") % 2
    here = pl.ds(pl.multiple_of(core * half, half), half)
    centre = pl.ds(pl.multiple_of(size + core * half, half), half)
    exact_ref[:half, :] = add(own_ref[here, :], inner_ref[1 - core, here, :])
    exact_ref[half:, :] = add(
        own_ref[centre, :], inner_ref[1 - core, centre, :], came_ref[0, here, :], came_ref[1, here, :]
    )
    out_ref[...] = exact_ref[...].astype(BF16)


def chip_sums(inner, own, came):
    vmem = pl.BlockSpec(memory_space=pltpu.VMEM)
    shape = came.shape[1:]
    out = (jax.ShapeDtypeStruct(shape, BF16), jax.ShapeDtypeStruct(shape, F32))
    return compiled(chip_kernel, out, [vmem] * 3, "chip_sums", flops=10**6)(inner, own, came)


def join_kernel(step, parts_ref, own_ref, out_ref, *exact_ref):
    mem = lax.axis_index("mem")
    other = 1 - (mem // 2 + mem % 2 + step) % 2
    total = own_ref[...] + parts_ref[other].astype(F32)
    out_ref[...] = total.astype(BF16)
    if exact_ref:
        exact_ref[0][...] = total


def join(step, parts, own):
    vmem = pl.BlockSpec(memory_space=pltpu.VMEM)
    out = [jax.ShapeDtypeStruct(own.shape, BF16), jax.ShapeDtypeStruct(own.shape, F32)][: 2 - step]
    kernel = functools.partial(join_kernel, step)
    return compiled(kernel, out, [vmem, vmem], "join", flops=10**6)(parts, own)


def middle_kernel(both_ref, out_ref):
    half = both_ref.shape[1] // 2
    out_ref[:half, :] = both_ref[0, :half, :]
    out_ref[half:, :] = both_ref[1, :half, :]


def middle_of(both):
    vmem = pl.BlockSpec(memory_space=pltpu.VMEM)
    out = jax.ShapeDtypeStruct(both.shape[1:], BF16)
    return compiled(middle_kernel, out, [vmem], "middle", flops=10**6)(both)


def pick(table, rows, block, chunks):
    levels = block.shape[0]
    picked = jnp.dot(table, one_hot(rows), preferred_element_type=F32)
    chunk = rows // LANES
    for i, k in enumerate(chunks):
        block = jnp.where(chunk == k, picked[i * levels : (i + 1) * levels], block)
    return block.astype(BF16)


def centre_kernel(rows_ref, middle_ref, out_ref):
    tiles, width = rows_ref.shape
    for tile in range(0, tiles, STEP):
        at = slice(tile * width, (tile + STEP) * width)
        none = jnp.zeros((out_ref.shape[0], STEP * width), F32)
        rows = some_rows(rows_ref, tile, STEP)
        out_ref[:, at] = pick(middle_ref[...], rows, none, CENTRE)


def centre_blocks(rows, middle):
    vmem = pl.BlockSpec(memory_space=pltpu.VMEM)
    out = jax.ShapeDtypeStruct((middle.shape[0] // CHUNKS, rows.size), BF16)
    return compiled(centre_kernel, out, [vmem, vmem], "centre_blocks")(rows, middle)


def fine_kernel(kept_ref, rows_ref, weights_ref, centre_ref, sides_ref, out_ref, block_ref):
    tiles, width, _ = weights_ref.shape
    kept = kept_ref[:1, :]
    sides = jnp.concatenate([sides_ref[0], sides_ref[1]], axis=0)
    for tile in range(0, tiles, STEP):
        at = slice(tile * width, (tile + STEP) * width)
        rows = some_rows(rows_ref, tile, STEP)
        block_ref[:, at] = pick(sides, rows, centre_ref[:, at].astype(F32), SIDES)
    for tile in range(tiles):
        at = slice(tile * width, (tile + 1) * width)
        fine = jnp.dot(block_ref[:, at], weights_ref[tile], preferred_element_type=F32)
        out_ref[:, at] = jnp.where(tile < kept, fine, 0.0).astype(BF16)


def fine_sum(kept, rows, weights, blocks, sides):
    vmem = pl.BlockSpec(memory_space=pltpu.VMEM)
    out = jax.ShapeDtypeStruct(blocks.shape, BF16)
    scratch = [pltpu.VMEM(blocks.shape, BF16)]
    return compiled(fine_kernel, out, [vmem] * 5, "fine_sum", scratch)(kept, rows, weights, blocks, sides)


def gradient_kernel(pert_ref, modes_ref, both_ref, out_ref):
    members, levels, points = pert_ref.shape
    half = both_ref.shape[1] // 2
    modes = jnp.concatenate([modes_ref[...], modes_ref[...]], axis=1)
    chunks = points // LANES
    for chunk in range(chunks):
        at = slice(chunk * LANES, (chunk + 1) * LANES)
        side, row = divmod(chunk * levels, half)
        adjoint = both_ref[side, half + row : half + row + levels, :].astype(F32)
        for k in range(members):
            product = pert_ref[k, :, at].astype(F32) * adjoint
            high = product.astype(BF16)
            low = (product - high.astype(F32)).astype(BF16)
            both = jnp.concatenate([high, low], axis=0)
            out_ref[k, :, at] = jnp.dot(modes, both, preferred_element_type=F32).astype(BF16)


def gradient(pert, modes, both):
    members, levels, points = pert.shape
    vmem = pl.BlockSpec(memory_space=pltpu.VMEM)
    out = jax.ShapeDtypeStruct((members, modes.shape[0], points), BF16)
    return compiled(gradient_kernel, out, [vmem, vmem, vmem], "gradient")(pert, modes, both)


def halo_route(bands, mems, near):
    route = []
    for b in range(bands):
        for m in range(mems):
            step = 1 - 2 * (m % 2)
            to = b + step
            if 0 <= to < bands:
                turn = 2 * step if to // near != b // near else 0
                route.append((b * mems + m, to * mems + (m + turn) % mems))
    return route


def chip_pairs(mems, step):
    chips = mems // 2
    return [
        [2 * chip + core, 2 * ((chip + 1) % chips) + core]
        for core in range(2)
        for chip in range(chips)
        if (chip + core + step) % 2 == 0
    ]


def shards(
    perturbations,
    mode_weights,
    vertical_modes,
    interp_weights,
    source_rows,
    live_tiles,
    fine_cotangent,
):
    bands, mems = lax.axis_size("band"), lax.axis_size("mem")
    pairs = [[m, m + 1] for m in range(0, mems, 2)]
    to_pair = functools.partial(lax.all_gather, axis_name="mem", axis_index_groups=pairs)
    to_bands = functools.partial(
        lax.ppermute, axis_name=("band", "mem"), perm=halo_route(bands, mems, NEAR)
    )

    modes = vertical_modes.T
    back, kept = back_blocks(live_tiles, fine_cotangent, interp_weights)
    came = to_bands(outward(to_pair(sides_sums(source_rows, back))))
    inner, own = inner_sums(perturbations, mode_weights, modes, source_rows, back)
    sums, own = chip_sums(to_pair(inner), own, to_pair(came))
    for step in range(2):
        parts = lax.all_gather(sums, "mem", axis_index_groups=chip_pairs(mems, step))
        sums, *own = join(step, parts, own)
        own = own[0] if own else None
    both = to_pair(sums)
    middle = middle_of(both)
    came = to_bands(middle)
    mode_gradient = gradient(perturbations, modes, both)
    blocks = centre_blocks(source_rows, middle)
    fine_increment = fine_sum(kept, source_rows, interp_weights, blocks, to_pair(came))
    return (fine_increment, mode_gradient)


def solution(mesh):
    placed = (
        P("mem", None, "band"),
        P("mem", None, "band"),
        P(),
        P(("band", "mem"), None, None),
        P(("band", "mem"), None),
        P("band"),
        P(None, ("band", "mem")),
    )
    return jax.shard_map(
        shards,
        mesh=mesh,
        in_specs=placed,
        out_specs=(P(None, ("band", "mem")), P("mem", None, "band")),
        check_vma=False,
    )
```

```python
import functools

import jax
import jax.numpy as jnp
from jax import lax
from jax.experimental import pallas as pl
from jax.experimental.pallas import tpu as pltpu
from jax.sharding import PartitionSpec as P

F32 = jnp.float32
BF16 = jnp.bfloat16
LANES = 256
BAND = 2048
CHUNKS = BAND // LANES
GROUP = 8
STEP = 4
NEAR = 4

CENTRE = range(CHUNKS, 2 * CHUNKS)
SIDES = [*range(CHUNKS), *range(2 * CHUNKS, 3 * CHUNKS)]


def compiled(kernel, out, in_specs, name, scratch=(), flops=2 * 10**9, mib=32, out_spec=None):
    vmem = pl.BlockSpec(memory_space=pltpu.VMEM)
    return pl.pallas_call(
        kernel,
        out_shape=out,
        in_specs=in_specs,
        out_specs=jax.tree.map(lambda _: out_spec or vmem, out),
        scratch_shapes=list(scratch),
        compiler_params=pltpu.CompilerParams(vmem_limit_bytes=int(mib * 2**20)),
        cost_estimate=pl.CostEstimate(flops=flops, bytes_accessed=2 * 10**6, transcendentals=0),
        name=name,
    )


def some_rows(rows_ref, tile, count):
    return jnp.concatenate([rows_ref[t : t + 1, :] for t in range(tile, tile + count)], axis=1)


def one_hot(rows):
    line = lax.broadcasted_iota(jnp.int32, (LANES, rows.shape[1]), 0).astype(F32).astype(BF16)
    column = (rows % LANES).astype(F32).astype(BF16)
    return jnp.where(column == line, jnp.ones((), BF16), jnp.zeros((), BF16))


def scattered(rows_ref, back_ref, chunks):
    tiles, width = rows_ref.shape
    zero = jnp.zeros((), BF16)
    total = None
    for start in range(0, tiles, GROUP):
        rows = some_rows(rows_ref, start, GROUP)
        chunk = (rows // LANES).astype(F32).astype(BF16)
        back = back_ref[:, start * width : (start + GROUP) * width]
        spread = jnp.concatenate([jnp.where(chunk == k, back, zero) for k in chunks], axis=0)
        part = lax.dot_general(
            spread, one_hot(rows), (((1,), (1,)), ((), ())), preferred_element_type=F32
        )
        total = part if total is None else total + part
    return total


def back_kernel(
    live_hbm, cot_hbm, weights_hbm, back_ref, kept_ref, live_ref, cot_ref, weights_ref, sems
):
    tiles, width, _ = weights_ref.shape
    copies = [
        pltpu.make_async_copy(live_hbm, live_ref, sems.at[0]),
        pltpu.make_async_copy(cot_hbm, cot_ref, sems.at[1]),
        pltpu.make_async_copy(weights_hbm, weights_ref, sems.at[2]),
    ]
    for copy in copies:
        copy.start()
    copies[0].wait()
    first = lax.axis_index("mem") * tiles
    live = live_ref[0, 0]
    kept_ref[...] = jnp.full(kept_ref.shape, live - first, jnp.int32)
    for copy in copies[1:]:
        copy.wait()
    for tile in range(tiles):
        at = slice(tile * width, (tile + 1) * width)
        back = lax.dot_general(
            weights_ref[tile], cot_ref[:, at], (((1,), (1,)), ((), ())), preferred_element_type=F32
        ).T
        back_ref[:, at] = jnp.where(first + tile < live, back, 0.0).astype(BF16)


def back_blocks(live, cot, weights):
    hbm = pl.BlockSpec(memory_space=pltpu.HBM)
    out = (
        jax.ShapeDtypeStruct(cot.shape, BF16),
        jax.ShapeDtypeStruct((8, weights.shape[2]), jnp.int32),
    )
    live = live.reshape(1, 1)
    scratch = [
        pltpu.SMEM(live.shape, live.dtype),
        pltpu.VMEM(cot.shape, cot.dtype),
        pltpu.VMEM(weights.shape, weights.dtype),
        pltpu.SemaphoreType.DMA((3,)),
    ]
    return compiled(back_kernel, out, [hbm] * 3, "back_blocks", scratch, mib=53.55)(live, cot, weights)


def sides_kernel(rows_ref, back_ref, give_ref, own_ref):
    core = lax.axis_index("mem") % 2
    both = scattered(rows_ref, back_ref, SIDES)
    below, above = both[: both.shape[0] // 2], both[both.shape[0] // 2 :]
    give_ref[...] = jnp.where(core == 0, below, above).astype(BF16)
    own_ref[...] = jnp.where(core == 0, above, below)


def sides_sums(rows, back):
    vmem = pl.BlockSpec(memory_space=pltpu.VMEM)
    shape = (CHUNKS * back.shape[0], LANES)
    out = (jax.ShapeDtypeStruct(shape, BF16), jax.ShapeDtypeStruct(shape, F32))
    return compiled(sides_kernel, out, [vmem, vmem], "sides_sums")(rows, back)


def inner_kernel(
    pert_ref, weights_ref, modes_ref, rows_ref, back_ref, give_ref, own_ref, sums_ref
):
    members, levels, points = pert_ref.shape
    for chunk in range(CHUNKS):
        at = slice(chunk * LANES, (chunk + 1) * LANES)
        total = jnp.zeros((levels, LANES), F32)
        for k in range(members):
            alpha = lax.dot_general(
                modes_ref[...],
                weights_ref[k, :, at],
                (((0,), (0,)), ((), ())),
                preferred_element_type=F32,
            )
            total = total + pert_ref[k, :, at].astype(F32) * alpha
        sums_ref[chunk * levels : (chunk + 1) * levels, :] = total
    sums_ref[CHUNKS * levels :, :] = scattered(rows_ref, back_ref, CENTRE)
    core = lax.axis_index("mem") % 2
    half = CHUNKS * levels // 2
    for i in range(2):
        at = slice(i * half, (i + 1) * half)
        give = pl.multiple_of((2 * i + 1 - core) * half, half)
        own = pl.multiple_of((2 * i + core) * half, half)
        give_ref[at, :] = sums_ref[pl.ds(give, half), :].astype(BF16)
        own_ref[at, :] = sums_ref[pl.ds(own, half), :]


def inner_sums(pert, mode_weights, modes, rows, back):
    vmem = pl.BlockSpec(memory_space=pltpu.VMEM)
    shape = (CHUNKS * pert.shape[1], LANES)
    out = (jax.ShapeDtypeStruct(shape, BF16), jax.ShapeDtypeStruct(shape, F32))
    scratch = [pltpu.VMEM((2 * shape[0], LANES), F32)]
    args = (pert, mode_weights, modes, rows, back)
    return compiled(inner_kernel, out, [vmem] * 5, "inner_sums", scratch)(*args)


def add(*refs):
    return functools.reduce(jnp.add, [ref[...].astype(F32) for ref in refs])


def outward_kernel(given_ref, own_ref, out_ref):
    core = lax.axis_index("mem") % 2
    out_ref[...] = add(own_ref, given_ref.at[1 - core]).astype(BF16)


def outward(given, own):
    vmem = pl.BlockSpec(memory_space=pltpu.VMEM)
    out = jax.ShapeDtypeStruct(own.shape, BF16)
    return compiled(outward_kernel, out, [vmem, vmem], "outward", flops=10**6)(given, own)


def chip_kernel(given_ref, own_ref, came_ref, out_ref, exact_ref):
    half = came_ref.shape[1] // 2
    core = lax.axis_index("mem") % 2
    here = pl.ds(pl.multiple_of(core * half, half), half)
    total = add(own_ref, given_ref.at[1 - core])
    exact_ref[:half, :] = total[:half]
    exact_ref[half:, :] = total[half:] + add(came_ref.at[0, here], came_ref.at[1, here])
    out_ref[...] = exact_ref[...].astype(BF16)


def chip_sums(given, own, came):
    vmem = pl.BlockSpec(memory_space=pltpu.VMEM)
    shape = came.shape[1:]
    out = (jax.ShapeDtypeStruct(shape, BF16), jax.ShapeDtypeStruct(shape, F32))
    return compiled(chip_kernel, out, [vmem] * 3, "chip_sums", flops=10**6)(given, own, came)


def join_kernel(step, parts_ref, own_ref, out_ref, *exact_ref):
    mem = lax.axis_index("mem")
    other = 1 - (mem // 2 + mem % 2 + step) % 2
    total = own_ref[...] + parts_ref[other].astype(F32)
    out_ref[...] = total.astype(BF16)
    if exact_ref:
        exact_ref[0][...] = total


def join(step, parts, own):
    vmem = pl.BlockSpec(memory_space=pltpu.VMEM)
    out = [jax.ShapeDtypeStruct(own.shape, BF16), jax.ShapeDtypeStruct(own.shape, F32)][: 2 - step]
    kernel = functools.partial(join_kernel, step)
    return compiled(kernel, out, [vmem, vmem], "join", flops=10**6)(parts, own)


def middle_kernel(both_ref, out_ref):
    half = both_ref.shape[1] // 2
    out_ref[:half, :] = both_ref[0, :half, :]
    out_ref[half:, :] = both_ref[1, :half, :]


def middle_of(both):
    vmem = pl.BlockSpec(memory_space=pltpu.VMEM)
    out = jax.ShapeDtypeStruct(both.shape[1:], BF16)
    return compiled(middle_kernel, out, [vmem], "middle", flops=10**6)(both)


def pick(table, rows, block, chunks):
    levels = block.shape[0]
    picked = jnp.dot(table, one_hot(rows), preferred_element_type=F32)
    chunk = rows // LANES
    for i, k in enumerate(chunks):
        block = jnp.where(chunk == k, picked[i * levels : (i + 1) * levels], block)
    return block.astype(BF16)


def centre_kernel(rows_ref, middle_ref, out_ref):
    tiles, width = rows_ref.shape
    for tile in range(0, tiles, STEP):
        at = slice(tile * width, (tile + STEP) * width)
        none = jnp.zeros((out_ref.shape[0], STEP * width), F32)
        rows = some_rows(rows_ref, tile, STEP)
        out_ref[:, at] = pick(middle_ref[...], rows, none, CENTRE)


def centre_blocks(rows, middle):
    vmem = pl.BlockSpec(memory_space=pltpu.VMEM)
    out = jax.ShapeDtypeStruct((middle.shape[0] // CHUNKS, rows.size), BF16)
    return compiled(centre_kernel, out, [vmem, vmem], "centre_blocks")(rows, middle)


def fine_kernel(
    kept_ref, rows_ref, weights_ref, centre_ref, sides_ref, out_hbm, block_ref, out_ref, sems
):
    tiles, width, _ = weights_ref.shape
    kept = kept_ref[:1, :]
    sides = jnp.concatenate([sides_ref[0], sides_ref[1]], axis=0)
    for tile in range(0, tiles, STEP):
        at = slice(tile * width, (tile + STEP) * width)
        rows = some_rows(rows_ref, tile, STEP)
        block_ref[:, at] = pick(sides, rows, centre_ref[:, at].astype(F32), SIDES)
    copies = []
    for start in range(0, tiles, GROUP):
        for tile in range(start, start + GROUP):
            at = slice(tile * width, (tile + 1) * width)
            fine = jnp.dot(block_ref[:, at], weights_ref[tile], preferred_element_type=F32)
            out_ref[:, at] = jnp.where(tile < kept, fine, 0.0).astype(BF16)
        part = pl.ds(start * width, GROUP * width)
        sem = sems.at[start // GROUP]
        copies.append(pltpu.make_async_copy(out_ref.at[:, part], out_hbm.at[:, part], sem))
        copies[-1].start()
    for copy in copies:
        copy.wait()


def fine_sum(kept, rows, weights, blocks, sides):
    vmem = pl.BlockSpec(memory_space=pltpu.VMEM)
    out = jax.ShapeDtypeStruct(blocks.shape, BF16)
    scratch = [
        pltpu.VMEM(blocks.shape, BF16),
        pltpu.VMEM(blocks.shape, BF16),
        pltpu.SemaphoreType.DMA((weights.shape[0] // GROUP,)),
    ]
    hbm = pl.BlockSpec(memory_space=pltpu.HBM)
    args = (kept, rows, weights, blocks, sides)
    return compiled(fine_kernel, out, [vmem] * 5, "fine_sum", scratch, out_spec=hbm)(*args)


def gradient_kernel(pert_ref, modes_ref, both_ref, out_ref):
    members, levels, points = pert_ref.shape
    half = both_ref.shape[1] // 2
    modes = jnp.concatenate([modes_ref[...], modes_ref[...]], axis=1)
    chunks = points // LANES
    for chunk in range(chunks):
        at = slice(chunk * LANES, (chunk + 1) * LANES)
        side, row = divmod(chunk * levels, half)
        adjoint = both_ref[side, half + row : half + row + levels, :].astype(F32)
        for k in range(members):
            product = pert_ref[k, :, at].astype(F32) * adjoint
            high = product.astype(BF16)
            low = (product - high.astype(F32)).astype(BF16)
            both = jnp.concatenate([high, low], axis=0)
            out_ref[k, :, at] = jnp.dot(modes, both, preferred_element_type=F32).astype(BF16)


def gradient(pert, modes, both):
    members, levels, points = pert.shape
    vmem = pl.BlockSpec(memory_space=pltpu.VMEM)
    out = jax.ShapeDtypeStruct((members, modes.shape[0], points), BF16)
    return compiled(gradient_kernel, out, [vmem, vmem, vmem], "gradient")(pert, modes, both)


def halo_route(bands, mems, near):
    route = []
    for b in range(bands):
        for m in range(mems):
            step = 1 - 2 * (m % 2)
            to = b + step
            if 0 <= to < bands:
                turn = 2 * step if to // near != b // near else 0
                route.append((b * mems + m, to * mems + (m + turn) % mems))
    return route


def chip_pairs(mems, step):
    chips = mems // 2
    return [
        [2 * chip + core, 2 * ((chip + 1) % chips) + core]
        for core in range(2)
        for chip in range(chips)
        if (chip + core + step) % 2 == 0
    ]


def shards(
    perturbations,
    mode_weights,
    vertical_modes,
    interp_weights,
    source_rows,
    live_tiles,
    fine_cotangent,
):
    bands, mems = lax.axis_size("band"), lax.axis_size("mem")
    pairs = [[m, m + 1] for m in range(0, mems, 2)]
    to_pair = functools.partial(lax.all_gather, axis_name="mem", axis_index_groups=pairs)
    to_bands = functools.partial(
        lax.ppermute, axis_name=("band", "mem"), perm=halo_route(bands, mems, NEAR)
    )

    modes = vertical_modes.T
    back, kept = back_blocks(live_tiles, fine_cotangent, interp_weights)
    give, own = sides_sums(source_rows, back)
    came = to_bands(outward(to_pair(give), own))
    give, own = inner_sums(perturbations, mode_weights, modes, source_rows, back)
    sums, own = chip_sums(to_pair(give), own, to_pair(came))
    for step in range(2):
        parts = lax.all_gather(sums, "mem", axis_index_groups=chip_pairs(mems, step))
        sums, *own = join(step, parts, own)
        own = own[0] if own else None
    both = to_pair(sums)
    middle = middle_of(both)
    came = to_bands(middle)
    mode_gradient = gradient(perturbations, modes, both)
    blocks = centre_blocks(source_rows, middle)
    fine_increment = fine_sum(kept, source_rows, interp_weights, blocks, to_pair(came))
    return (fine_increment, mode_gradient)


def solution(mesh):
    placed = (
        P("mem", None, "band"),
        P("mem", None, "band"),
        P(),
        P(("band", "mem"), None, None),
        P(("band", "mem"), None),
        P("band"),
        P(None, ("band", "mem")),
    )
    return jax.shard_map(
        shards,
        mesh=mesh,
        in_specs=placed,
        out_specs=(P(None, ("band", "mem")), P("mem", None, "band")),
        check_vma=False,
    )
```

```python
import functools

import jax
import jax.numpy as jnp
from jax import lax
from jax.experimental import pallas as pl
from jax.experimental.pallas import tpu as pltpu
from jax.sharding import PartitionSpec as P

F32 = jnp.float32
BF16 = jnp.bfloat16
LANES = 256
BAND = 2048
CHUNKS = BAND // LANES
GROUP = 8
STEP = 4
NEAR = 4

CENTRE = range(CHUNKS, 2 * CHUNKS)
SIDES = [*range(CHUNKS), *range(2 * CHUNKS, 3 * CHUNKS)]


def compiled(kernel, out, in_specs, name, scratch=(), flops=2 * 10**9, mib=32, out_spec=None):
    vmem = pl.BlockSpec(memory_space=pltpu.VMEM)
    return pl.pallas_call(
        kernel,
        out_shape=out,
        in_specs=in_specs,
        out_specs=jax.tree.map(lambda _: out_spec or vmem, out),
        scratch_shapes=list(scratch),
        compiler_params=pltpu.CompilerParams(vmem_limit_bytes=int(mib * 2**20)),
        cost_estimate=pl.CostEstimate(flops=flops, bytes_accessed=2 * 10**6, transcendentals=0),
        name=name,
    )


def some_rows(rows_ref, tile, count):
    return jnp.concatenate([rows_ref[t : t + 1, :] for t in range(tile, tile + count)], axis=1)


def one_hot(rows):
    line = lax.broadcasted_iota(jnp.int32, (LANES, rows.shape[1]), 0).astype(F32).astype(BF16)
    column = (rows % LANES).astype(F32).astype(BF16)
    return jnp.where(column == line, jnp.ones((), BF16), jnp.zeros((), BF16))


def scattered(rows_ref, back_ref, chunks):
    tiles, width = rows_ref.shape
    zero = jnp.zeros((), BF16)
    total = None
    for start in range(0, tiles, GROUP):
        rows = some_rows(rows_ref, start, GROUP)
        chunk = (rows // LANES).astype(F32).astype(BF16)
        back = back_ref[:, start * width : (start + GROUP) * width]
        spread = jnp.concatenate([jnp.where(chunk == k, back, zero) for k in chunks], axis=0)
        part = lax.dot_general(
            spread, one_hot(rows), (((1,), (1,)), ((), ())), preferred_element_type=F32
        )
        total = part if total is None else total + part
    return total


def back_kernel(
    live_hbm, cot_hbm, weights_hbm, back_ref, kept_ref, live_ref, cot_ref, weights_ref, sems
):
    tiles, width, _ = weights_ref.shape
    copies = [
        pltpu.make_async_copy(live_hbm, live_ref, sems.at[0]),
        pltpu.make_async_copy(cot_hbm, cot_ref, sems.at[1]),
        pltpu.make_async_copy(weights_hbm, weights_ref, sems.at[2]),
    ]
    for copy in copies:
        copy.start()
    copies[0].wait()
    first = lax.axis_index("mem") * tiles
    live = live_ref[0, 0]
    kept_ref[...] = jnp.full(kept_ref.shape, live - first, jnp.int32)
    for copy in copies[1:]:
        copy.wait()
    for tile in range(tiles):
        at = slice(tile * width, (tile + 1) * width)
        back = lax.dot_general(
            weights_ref[tile], cot_ref[:, at], (((1,), (1,)), ((), ())), preferred_element_type=F32
        ).T
        back_ref[:, at] = jnp.where(first + tile < live, back, 0.0).astype(BF16)


def back_blocks(live, cot, weights):
    hbm = pl.BlockSpec(memory_space=pltpu.HBM)
    out = (
        jax.ShapeDtypeStruct(cot.shape, BF16),
        jax.ShapeDtypeStruct((8, weights.shape[2]), jnp.int32),
    )
    live = live.reshape(1, 1)
    scratch = [
        pltpu.SMEM(live.shape, live.dtype),
        pltpu.VMEM(cot.shape, cot.dtype),
        pltpu.VMEM(weights.shape, weights.dtype),
        pltpu.SemaphoreType.DMA((3,)),
    ]
    return compiled(back_kernel, out, [hbm] * 3, "back_blocks", scratch, mib=53.55)(live, cot, weights)


def sides_kernel(rows_ref, back_ref, give_ref, own_ref):
    core = lax.axis_index("mem") % 2
    both = scattered(rows_ref, back_ref, SIDES)
    below, above = both[: both.shape[0] // 2], both[both.shape[0] // 2 :]
    give_ref[...] = jnp.where(core == 0, below, above).astype(BF16)
    own_ref[...] = jnp.where(core == 0, above, below)


def sides_sums(rows, back):
    vmem = pl.BlockSpec(memory_space=pltpu.VMEM)
    shape = (CHUNKS * back.shape[0], LANES)
    out = (jax.ShapeDtypeStruct(shape, BF16), jax.ShapeDtypeStruct(shape, F32))
    return compiled(sides_kernel, out, [vmem, vmem], "sides_sums")(rows, back)


def inner_kernel(
    pert_ref, weights_ref, modes_ref, rows_ref, back_ref, give_ref, own_ref, sums_ref
):
    members, levels, points = pert_ref.shape
    for chunk in range(CHUNKS):
        at = slice(chunk * LANES, (chunk + 1) * LANES)
        total = jnp.zeros((levels, LANES), F32)
        for k in range(members):
            alpha = lax.dot_general(
                modes_ref[...],
                weights_ref[k, :, at],
                (((0,), (0,)), ((), ())),
                preferred_element_type=F32,
            )
            total = total + pert_ref[k, :, at].astype(F32) * alpha
        sums_ref[chunk * levels : (chunk + 1) * levels, :] = total
    sums_ref[CHUNKS * levels :, :] = scattered(rows_ref, back_ref, CENTRE)
    core = lax.axis_index("mem") % 2
    half = CHUNKS * levels // 2
    for i in range(2):
        at = slice(i * half, (i + 1) * half)
        give = pl.multiple_of((2 * i + 1 - core) * half, half)
        own = pl.multiple_of((2 * i + core) * half, half)
        give_ref[at, :] = sums_ref[pl.ds(give, half), :].astype(BF16)
        own_ref[at, :] = sums_ref[pl.ds(own, half), :]


def inner_sums(pert, mode_weights, modes, rows, back):
    vmem = pl.BlockSpec(memory_space=pltpu.VMEM)
    shape = (CHUNKS * pert.shape[1], LANES)
    out = (jax.ShapeDtypeStruct(shape, BF16), jax.ShapeDtypeStruct(shape, F32))
    scratch = [pltpu.VMEM((2 * shape[0], LANES), F32)]
    args = (pert, mode_weights, modes, rows, back)
    return compiled(inner_kernel, out, [vmem] * 5, "inner_sums", scratch)(*args)


def add(*refs):
    return functools.reduce(jnp.add, [ref[...].astype(F32) for ref in refs])


def outward_kernel(given_ref, own_ref, out_ref):
    core = lax.axis_index("mem") % 2
    out_ref[...] = add(own_ref, given_ref.at[1 - core]).astype(BF16)


def outward(given, own):
    vmem = pl.BlockSpec(memory_space=pltpu.VMEM)
    out = jax.ShapeDtypeStruct(own.shape, BF16)
    return compiled(outward_kernel, out, [vmem, vmem], "outward", flops=10**6)(given, own)


def chip_kernel(given_ref, own_ref, came_ref, out_ref, exact_ref):
    half = came_ref.shape[1] // 2
    core = lax.axis_index("mem") % 2
    here = pl.ds(pl.multiple_of(core * half, half), half)
    total = add(own_ref, given_ref.at[1 - core])
    exact_ref[:half, :] = total[:half]
    exact_ref[half:, :] = total[half:] + add(came_ref.at[0, here], came_ref.at[1, here])
    out_ref[...] = exact_ref[...].astype(BF16)


def chip_sums(given, own, came):
    vmem = pl.BlockSpec(memory_space=pltpu.VMEM)
    shape = came.shape[1:]
    out = (jax.ShapeDtypeStruct(shape, BF16), jax.ShapeDtypeStruct(shape, F32))
    return compiled(chip_kernel, out, [vmem] * 3, "chip_sums", flops=10**6)(given, own, came)


def join_kernel(step, parts_ref, own_ref, out_ref, *exact_ref):
    mem = lax.axis_index("mem")
    other = 1 - (mem // 2 + mem % 2 + step) % 2
    total = own_ref[...] + parts_ref[other].astype(F32)
    out_ref[...] = total.astype(BF16)
    if exact_ref:
        exact_ref[0][...] = total


def join(step, parts, own):
    vmem = pl.BlockSpec(memory_space=pltpu.VMEM)
    out = [jax.ShapeDtypeStruct(own.shape, BF16), jax.ShapeDtypeStruct(own.shape, F32)][: 2 - step]
    kernel = functools.partial(join_kernel, step)
    return compiled(kernel, out, [vmem, vmem], "join", flops=10**6)(parts, own)


def middle_kernel(both_ref, out_ref):
    half = both_ref.shape[1] // 2
    out_ref[:half, :] = both_ref[0, :half, :]
    out_ref[half:, :] = both_ref[1, :half, :]


def middle_of(both):
    vmem = pl.BlockSpec(memory_space=pltpu.VMEM)
    out = jax.ShapeDtypeStruct(both.shape[1:], BF16)
    return compiled(middle_kernel, out, [vmem], "middle", flops=10**6)(both)


def pick(table, rows, hot, block, chunks):
    levels = block.shape[0]
    picked = jnp.dot(table, hot, preferred_element_type=F32)
    chunk = rows // LANES
    for i, k in enumerate(chunks):
        block = jnp.where(chunk == k, picked[i * levels : (i + 1) * levels], block)
    return block.astype(BF16)


def centre_kernel(rows_ref, middle_ref, out_ref, hot_ref):
    tiles, width = rows_ref.shape
    for tile in range(0, tiles, STEP):
        at = slice(tile * width, (tile + STEP) * width)
        none = jnp.zeros((out_ref.shape[0], STEP * width), F32)
        rows = some_rows(rows_ref, tile, STEP)
        hot = one_hot(rows)
        hot_ref[:, at] = hot
        out_ref[:, at] = pick(middle_ref[...], rows, hot, none, CENTRE)


def centre_blocks(rows, middle):
    vmem = pl.BlockSpec(memory_space=pltpu.VMEM)
    out = (
        jax.ShapeDtypeStruct((middle.shape[0] // CHUNKS, rows.size), BF16),
        jax.ShapeDtypeStruct((LANES, rows.size), BF16),
    )
    return compiled(centre_kernel, out, [vmem, vmem], "centre_blocks")(rows, middle)


def fine_kernel(
    kept_ref, rows_ref, weights_ref, centre_ref, hot_ref, sides_ref, out_hbm, block_ref, out_ref, sems
):
    tiles, width, _ = weights_ref.shape
    kept = kept_ref[:1, :]
    sides = jnp.concatenate([sides_ref[0], sides_ref[1]], axis=0)
    for tile in range(0, tiles, STEP):
        at = slice(tile * width, (tile + STEP) * width)
        rows = some_rows(rows_ref, tile, STEP)
        block_ref[:, at] = pick(sides, rows, hot_ref[:, at], centre_ref[:, at].astype(F32), SIDES)
    copies = []
    for start in range(0, tiles, GROUP):
        for tile in range(start, start + GROUP):
            at = slice(tile * width, (tile + 1) * width)
            fine = jnp.dot(block_ref[:, at], weights_ref[tile], preferred_element_type=F32)
            out_ref[:, at] = jnp.where(tile < kept, fine, 0.0).astype(BF16)
        part = pl.ds(start * width, GROUP * width)
        sem = sems.at[start // GROUP]
        copies.append(pltpu.make_async_copy(out_ref.at[:, part], out_hbm.at[:, part], sem))
        copies[-1].start()
    for copy in copies:
        copy.wait()


def fine_sum(kept, rows, weights, blocks, hot, sides):
    vmem = pl.BlockSpec(memory_space=pltpu.VMEM)
    out = jax.ShapeDtypeStruct(blocks.shape, BF16)
    scratch = [
        pltpu.VMEM(blocks.shape, BF16),
        pltpu.VMEM(blocks.shape, BF16),
        pltpu.SemaphoreType.DMA((weights.shape[0] // GROUP,)),
    ]
    hbm = pl.BlockSpec(memory_space=pltpu.HBM)
    args = (kept, rows, weights, blocks, hot, sides)
    return compiled(fine_kernel, out, [vmem] * 6, "fine_sum", scratch, out_spec=hbm)(*args)


def gradient_kernel(pert_ref, modes_ref, both_ref, out_ref):
    members, levels, points = pert_ref.shape
    half = both_ref.shape[1] // 2
    modes = jnp.concatenate([modes_ref[...], modes_ref[...]], axis=1)
    chunks = points // LANES
    for chunk in range(chunks):
        at = slice(chunk * LANES, (chunk + 1) * LANES)
        side, row = divmod(chunk * levels, half)
        adjoint = both_ref[side, half + row : half + row + levels, :].astype(F32)
        for k in range(members):
            product = pert_ref[k, :, at].astype(F32) * adjoint
            high = product.astype(BF16)
            low = (product - high.astype(F32)).astype(BF16)
            both = jnp.concatenate([high, low], axis=0)
            out_ref[k, :, at] = jnp.dot(modes, both, preferred_element_type=F32).astype(BF16)


def gradient(pert, modes, both):
    members, levels, points = pert.shape
    vmem = pl.BlockSpec(memory_space=pltpu.VMEM)
    out = jax.ShapeDtypeStruct((members, modes.shape[0], points), BF16)
    return compiled(gradient_kernel, out, [vmem, vmem, vmem], "gradient")(pert, modes, both)


def halo_route(bands, mems, near):
    route = []
    for b in range(bands):
        for m in range(mems):
            step = 1 - 2 * (m % 2)
            to = b + step
            if 0 <= to < bands:
                turn = 2 * step if to // near != b // near else 0
                route.append((b * mems + m, to * mems + (m + turn) % mems))
    return route


def chip_pairs(mems, step):
    chips = mems // 2
    return [
        [2 * chip + core, 2 * ((chip + 1) % chips) + core]
        for core in range(2)
        for chip in range(chips)
        if (chip + core + step) % 2 == 0
    ]


def shards(
    perturbations,
    mode_weights,
    vertical_modes,
    interp_weights,
    source_rows,
    live_tiles,
    fine_cotangent,
):
    bands, mems = lax.axis_size("band"), lax.axis_size("mem")
    pairs = [[m, m + 1] for m in range(0, mems, 2)]
    to_pair = functools.partial(lax.all_gather, axis_name="mem", axis_index_groups=pairs)
    to_bands = functools.partial(
        lax.ppermute, axis_name=("band", "mem"), perm=halo_route(bands, mems, NEAR)
    )

    modes = vertical_modes.T
    back, kept = back_blocks(live_tiles, fine_cotangent, interp_weights)
    give, own = sides_sums(source_rows, back)
    came = to_bands(outward(to_pair(give), own))
    give, own = inner_sums(perturbations, mode_weights, modes, source_rows, back)
    sums, own = chip_sums(to_pair(give), own, to_pair(came))
    for step in range(2):
        parts = lax.all_gather(sums, "mem", axis_index_groups=chip_pairs(mems, step))
        sums, *own = join(step, parts, own)
        own = own[0] if own else None
    both = to_pair(sums)
    middle = middle_of(both)
    came = to_bands(middle)
    mode_gradient = gradient(perturbations, modes, both)
    blocks, hot = centre_blocks(source_rows, middle)
    fine_increment = fine_sum(kept, source_rows, interp_weights, blocks, hot, to_pair(came))
    return (fine_increment, mode_gradient)


def solution(mesh):
    placed = (
        P("mem", None, "band"),
        P("mem", None, "band"),
        P(),
        P(("band", "mem"), None, None),
        P(("band", "mem"), None),
        P("band"),
        P(None, ("band", "mem")),
    )
    return jax.shard_map(
        shards,
        mesh=mesh,
        in_specs=placed,
        out_specs=(P(None, ("band", "mem")), P("mem", None, "band")),
        check_vma=False,
    )
```

```python
import functools

import jax
import jax.numpy as jnp
from jax import lax
from jax.experimental import pallas as pl
from jax.experimental.pallas import tpu as pltpu
from jax.sharding import PartitionSpec as P

F32 = jnp.float32
BF16 = jnp.bfloat16
LANES = 256
BAND = 2048
CHUNKS = BAND // LANES
GROUP = 8
STEP = 4
NEAR = 4

CENTRE = range(CHUNKS, 2 * CHUNKS)
SIDES = [*range(CHUNKS), *range(2 * CHUNKS, 3 * CHUNKS)]


def compiled(kernel, out, in_specs, name, scratch=(), flops=2 * 10**9, mib=32, out_spec=None):
    vmem = pl.BlockSpec(memory_space=pltpu.VMEM)
    return pl.pallas_call(
        kernel,
        out_shape=out,
        in_specs=in_specs,
        out_specs=jax.tree.map(lambda _: out_spec or vmem, out),
        scratch_shapes=list(scratch),
        compiler_params=pltpu.CompilerParams(vmem_limit_bytes=int(mib * 2**20)),
        cost_estimate=pl.CostEstimate(flops=flops, bytes_accessed=2 * 10**6, transcendentals=0),
        name=name,
    )


def some_rows(rows_ref, tile, count):
    return jnp.concatenate([rows_ref[t : t + 1, :] for t in range(tile, tile + count)], axis=1)


def one_hot(rows):
    line = lax.broadcasted_iota(jnp.int32, (LANES, rows.shape[1]), 0).astype(F32).astype(BF16)
    column = (rows % LANES).astype(F32).astype(BF16)
    return jnp.where(column == line, jnp.ones((), BF16), jnp.zeros((), BF16))


def scattered(rows_ref, back_ref, chunks):
    tiles, width = rows_ref.shape
    zero = jnp.zeros((), BF16)
    total = None
    for start in range(0, tiles, GROUP):
        rows = some_rows(rows_ref, start, GROUP)
        chunk = (rows // LANES).astype(F32).astype(BF16)
        back = back_ref[:, start * width : (start + GROUP) * width]
        spread = jnp.concatenate([jnp.where(chunk == k, back, zero) for k in chunks], axis=0)
        part = lax.dot_general(
            spread, one_hot(rows), (((1,), (1,)), ((), ())), preferred_element_type=F32
        )
        total = part if total is None else total + part
    return total


def back_kernel(
    live_hbm, cot_hbm, weights_hbm, back_ref, kept_ref, live_ref, cot_ref, weights_ref, sems
):
    tiles, width, _ = weights_ref.shape
    copies = [
        pltpu.make_async_copy(live_hbm, live_ref, sems.at[0]),
        pltpu.make_async_copy(cot_hbm, cot_ref, sems.at[1]),
        pltpu.make_async_copy(weights_hbm, weights_ref, sems.at[2]),
    ]
    for copy in copies:
        copy.start()
    copies[0].wait()
    first = lax.axis_index("mem") * tiles
    live = live_ref[0, 0]
    kept_ref[...] = jnp.full(kept_ref.shape, live - first, jnp.int32)
    for copy in copies[1:]:
        copy.wait()
    for tile in range(tiles):
        at = slice(tile * width, (tile + 1) * width)
        back = lax.dot_general(
            weights_ref[tile], cot_ref[:, at], (((1,), (1,)), ((), ())), preferred_element_type=F32
        )
        back_ref[:, at] = jnp.where(first + tile < live, back, 0.0).astype(BF16).T


def back_blocks(live, cot, weights):
    hbm = pl.BlockSpec(memory_space=pltpu.HBM)
    out = (
        jax.ShapeDtypeStruct(cot.shape, BF16),
        jax.ShapeDtypeStruct((8, weights.shape[2]), jnp.int32),
    )
    live = live.reshape(1, 1)
    scratch = [
        pltpu.SMEM(live.shape, live.dtype),
        pltpu.VMEM(cot.shape, cot.dtype),
        pltpu.VMEM(weights.shape, weights.dtype),
        pltpu.SemaphoreType.DMA((3,)),
    ]
    return compiled(back_kernel, out, [hbm] * 3, "back_blocks", scratch, mib=53.55)(live, cot, weights)


def sides_kernel(rows_ref, back_ref, give_ref, own_ref):
    core = lax.axis_index("mem") % 2
    both = scattered(rows_ref, back_ref, SIDES)
    below, above = both[: both.shape[0] // 2], both[both.shape[0] // 2 :]
    give_ref[...] = jnp.where(core == 0, below, above).astype(BF16)
    own_ref[...] = jnp.where(core == 0, above, below)


def sides_sums(rows, back):
    vmem = pl.BlockSpec(memory_space=pltpu.VMEM)
    shape = (CHUNKS * back.shape[0], LANES)
    out = (jax.ShapeDtypeStruct(shape, BF16), jax.ShapeDtypeStruct(shape, F32))
    return compiled(sides_kernel, out, [vmem, vmem], "sides_sums")(rows, back)


def inner_kernel(
    pert_ref, weights_ref, modes_ref, rows_ref, back_ref, give_ref, own_ref, sums_ref
):
    members, levels, points = pert_ref.shape
    for chunk in range(CHUNKS):
        at = slice(chunk * LANES, (chunk + 1) * LANES)
        total = jnp.zeros((levels, LANES), F32)
        for k in range(members):
            alpha = lax.dot_general(
                modes_ref[...],
                weights_ref[k, :, at],
                (((0,), (0,)), ((), ())),
                preferred_element_type=F32,
            )
            total = total + pert_ref[k, :, at].astype(F32) * alpha
        sums_ref[chunk * levels : (chunk + 1) * levels, :] = total
    sums_ref[CHUNKS * levels :, :] = scattered(rows_ref, back_ref, CENTRE)
    core = lax.axis_index("mem") % 2
    half = CHUNKS * levels // 2
    for i in range(2):
        at = slice(i * half, (i + 1) * half)
        give = pl.multiple_of((2 * i + 1 - core) * half, half)
        own = pl.multiple_of((2 * i + core) * half, half)
        give_ref[at, :] = sums_ref[pl.ds(give, half), :].astype(BF16)
        own_ref[at, :] = sums_ref[pl.ds(own, half), :]


def inner_sums(pert, mode_weights, modes, rows, back):
    vmem = pl.BlockSpec(memory_space=pltpu.VMEM)
    shape = (CHUNKS * pert.shape[1], LANES)
    out = (jax.ShapeDtypeStruct(shape, BF16), jax.ShapeDtypeStruct(shape, F32))
    scratch = [pltpu.VMEM((2 * shape[0], LANES), F32)]
    args = (pert, mode_weights, modes, rows, back)
    return compiled(inner_kernel, out, [vmem] * 5, "inner_sums", scratch)(*args)


def add(*refs):
    return functools.reduce(jnp.add, [ref[...].astype(F32) for ref in refs])


def outward_kernel(given_ref, own_ref, out_ref):
    core = lax.axis_index("mem") % 2
    out_ref[...] = add(own_ref, given_ref.at[1 - core]).astype(BF16)


def outward(given, own):
    vmem = pl.BlockSpec(memory_space=pltpu.VMEM)
    out = jax.ShapeDtypeStruct(own.shape, BF16)
    return compiled(outward_kernel, out, [vmem, vmem], "outward", flops=10**6)(given, own)


def chip_kernel(given_ref, own_ref, came_ref, out_ref, exact_ref):
    half = came_ref.shape[1] // 2
    core = lax.axis_index("mem") % 2
    here = pl.ds(pl.multiple_of(core * half, half), half)
    total = add(own_ref, given_ref.at[1 - core])
    exact_ref[:half, :] = total[:half]
    exact_ref[half:, :] = total[half:] + add(came_ref.at[0, here], came_ref.at[1, here])
    out_ref[...] = exact_ref[...].astype(BF16)


def chip_sums(given, own, came):
    vmem = pl.BlockSpec(memory_space=pltpu.VMEM)
    shape = came.shape[1:]
    out = (jax.ShapeDtypeStruct(shape, BF16), jax.ShapeDtypeStruct(shape, F32))
    return compiled(chip_kernel, out, [vmem] * 3, "chip_sums", flops=10**6)(given, own, came)


def join_kernel(step, parts_ref, own_ref, out_ref, *exact_ref):
    mem = lax.axis_index("mem")
    other = 1 - (mem // 2 + mem % 2 + step) % 2
    total = own_ref[...] + parts_ref[other].astype(F32)
    out_ref[...] = total.astype(BF16)
    if exact_ref:
        exact_ref[0][...] = total


def join(step, parts, own):
    vmem = pl.BlockSpec(memory_space=pltpu.VMEM)
    out = [jax.ShapeDtypeStruct(own.shape, BF16), jax.ShapeDtypeStruct(own.shape, F32)][: 2 - step]
    kernel = functools.partial(join_kernel, step)
    return compiled(kernel, out, [vmem, vmem], "join", flops=10**6)(parts, own)


def middle_kernel(both_ref, out_ref):
    half = both_ref.shape[1] // 2
    out_ref[:half, :] = both_ref[0, :half, :]
    out_ref[half:, :] = both_ref[1, :half, :]


def middle_of(both):
    vmem = pl.BlockSpec(memory_space=pltpu.VMEM)
    out = jax.ShapeDtypeStruct(both.shape[1:], BF16)
    return compiled(middle_kernel, out, [vmem], "middle", flops=10**6)(both)


def pick(table, rows, block, chunks):
    levels = block.shape[0]
    picked = jnp.dot(table, one_hot(rows), preferred_element_type=F32)
    chunk = rows // LANES
    for i, k in enumerate(chunks):
        block = jnp.where(chunk == k, picked[i * levels : (i + 1) * levels], block)
    return block.astype(BF16)


def centre_kernel(rows_ref, middle_ref, out_ref):
    tiles, width = rows_ref.shape
    for tile in range(0, tiles, STEP):
        at = slice(tile * width, (tile + STEP) * width)
        none = jnp.zeros((out_ref.shape[0], STEP * width), F32)
        rows = some_rows(rows_ref, tile, STEP)
        out_ref[:, at] = pick(middle_ref[...], rows, none, CENTRE)


def centre_blocks(rows, middle):
    vmem = pl.BlockSpec(memory_space=pltpu.VMEM)
    out = jax.ShapeDtypeStruct((middle.shape[0] // CHUNKS, rows.size), BF16)
    return compiled(centre_kernel, out, [vmem, vmem], "centre_blocks")(rows, middle)


def fine_kernel(
    kept_ref, rows_ref, weights_ref, centre_ref, sides_ref, out_hbm, block_ref, out_ref, sems
):
    tiles, width, _ = weights_ref.shape
    kept = kept_ref[:1, :]
    sides = jnp.concatenate([sides_ref[0], sides_ref[1]], axis=0)
    for tile in range(0, tiles, STEP):
        at = slice(tile * width, (tile + STEP) * width)
        rows = some_rows(rows_ref, tile, STEP)
        block_ref[:, at] = pick(sides, rows, centre_ref[:, at].astype(F32), SIDES)
    copies = []
    for start in range(0, tiles, GROUP):
        for tile in range(start, start + GROUP):
            at = slice(tile * width, (tile + 1) * width)
            fine = jnp.dot(block_ref[:, at], weights_ref[tile], preferred_element_type=F32)
            out_ref[:, at] = jnp.where(tile < kept, fine, 0.0).astype(BF16)
        part = pl.ds(start * width, GROUP * width)
        sem = sems.at[start // GROUP]
        copies.append(pltpu.make_async_copy(out_ref.at[:, part], out_hbm.at[:, part], sem))
        copies[-1].start()
    for copy in copies:
        copy.wait()


def fine_sum(kept, rows, weights, blocks, sides):
    vmem = pl.BlockSpec(memory_space=pltpu.VMEM)
    out = jax.ShapeDtypeStruct(blocks.shape, BF16)
    scratch = [
        pltpu.VMEM(blocks.shape, BF16),
        pltpu.VMEM(blocks.shape, BF16),
        pltpu.SemaphoreType.DMA((weights.shape[0] // GROUP,)),
    ]
    hbm = pl.BlockSpec(memory_space=pltpu.HBM)
    args = (kept, rows, weights, blocks, sides)
    return compiled(fine_kernel, out, [vmem] * 5, "fine_sum", scratch, out_spec=hbm)(*args)


def gradient_kernel(pert_ref, modes_ref, both_ref, out_ref):
    members, levels, points = pert_ref.shape
    half = both_ref.shape[1] // 2
    modes = jnp.concatenate([modes_ref[...], modes_ref[...]], axis=1)
    chunks = points // LANES
    for chunk in range(chunks):
        at = slice(chunk * LANES, (chunk + 1) * LANES)
        side, row = divmod(chunk * levels, half)
        adjoint = both_ref[side, half + row : half + row + levels, :].astype(F32)
        for k in range(members):
            product = pert_ref[k, :, at].astype(F32) * adjoint
            high = product.astype(BF16)
            low = (product - high.astype(F32)).astype(BF16)
            both = jnp.concatenate([high, low], axis=0)
            out_ref[k, :, at] = jnp.dot(modes, both, preferred_element_type=F32).astype(BF16)


def gradient(pert, modes, both):
    members, levels, points = pert.shape
    vmem = pl.BlockSpec(memory_space=pltpu.VMEM)
    out = jax.ShapeDtypeStruct((members, modes.shape[0], points), BF16)
    return compiled(gradient_kernel, out, [vmem, vmem, vmem], "gradient")(pert, modes, both)


def halo_route(bands, mems, near):
    route = []
    for b in range(bands):
        for m in range(mems):
            step = 1 - 2 * (m % 2)
            to = b + step
            if 0 <= to < bands:
                turn = 2 * step if to // near != b // near else 0
                route.append((b * mems + m, to * mems + (m + turn) % mems))
    return route


def chip_pairs(mems, step):
    chips = mems // 2
    return [
        [2 * chip + core, 2 * ((chip + 1) % chips) + core]
        for core in range(2)
        for chip in range(chips)
        if (chip + core + step) % 2 == 0
    ]


def shards(
    perturbations,
    mode_weights,
    vertical_modes,
    interp_weights,
    source_rows,
    live_tiles,
    fine_cotangent,
):
    bands, mems = lax.axis_size("band"), lax.axis_size("mem")
    pairs = [[m, m + 1] for m in range(0, mems, 2)]
    to_pair = functools.partial(lax.all_gather, axis_name="mem", axis_index_groups=pairs)
    to_bands = functools.partial(
        lax.ppermute, axis_name=("band", "mem"), perm=halo_route(bands, mems, NEAR)
    )

    modes = vertical_modes.T
    back, kept = back_blocks(live_tiles, fine_cotangent, interp_weights)
    give, own = sides_sums(source_rows, back)
    came = to_bands(outward(to_pair(give), own))
    give, own = inner_sums(perturbations, mode_weights, modes, source_rows, back)
    sums, own = chip_sums(to_pair(give), own, to_pair(came))
    for step in range(2):
        parts = lax.all_gather(sums, "mem", axis_index_groups=chip_pairs(mems, step))
        sums, *own = join(step, parts, own)
        own = own[0] if own else None
    both = to_pair(sums)
    middle = middle_of(both)
    came = to_bands(middle)
    mode_gradient = gradient(perturbations, modes, both)
    blocks = centre_blocks(source_rows, middle)
    fine_increment = fine_sum(kept, source_rows, interp_weights, blocks, to_pair(came))
    return (fine_increment, mode_gradient)


def solution(mesh):
    placed = (
        P("mem", None, "band"),
        P("mem", None, "band"),
        P(),
        P(("band", "mem"), None, None),
        P(("band", "mem"), None),
        P("band"),
        P(None, ("band", "mem")),
    )
    return jax.shard_map(
        shards,
        mesh=mesh,
        in_specs=placed,
        out_specs=(P(None, ("band", "mem")), P("mem", None, "band")),
        check_vma=False,
    )
```
